1024 devices in a mesh: grp: 128 (over y, z_lo, x), tp: 8 (over z_hi, core).
Axes of the slice: x: 8, y: 8, z: 8 (z_hi: 4, z_lo: 2; z = z_hi * 2 + z_lo), core: 2. Of those that a mesh axis runs over, the one named last changes fastest.
Arguments:
- tokens: bfloat16 [1024, 4096], P('grp', 'tp'), may hold values from -6 to 6
- expert_ids: int32 [1024, 8], replicated, may hold values from 0 to 127, all different within a row; in each aligned block of 1024 rows (0 to 1023, 1024 to 2047, ...) at most 160 rows name the same one
- route_weight: float32 [1024, 8], replicated, may hold values from 0.1 to 1
- owner: int32 [128], replicated, may hold values from 0 to 127, each once
- gate_weight: bfloat16 [128, 4096, 1024], P('grp', 'tp'), may hold values from -0.09375 to 0.09375
- up_weight: bfloat16 [128, 4096, 1024], P('grp', 'tp'), may hold values from -0.09375 to 0.09375
- down_weight: bfloat16 [128, 1024, 4096], P('grp', None, 'tp'), may hold values from -0.1875 to 0.1875
Outputs:
- mixed: bfloat16 [1024, 4096], P('grp', 'tp')
The draws below stay inside these ranges and needn't reach their ends.
Inputs may be any that keep to these rules, and one draw needn't show every extreme that they name: `expert_ids`: each row names 8 different experts; no expert is named by more than 160 rows, a bound that some block reaches. `owner`: A permutation: every group owns exactly one expert.
All inputs are finite; a program needn't handle non-finite values.
Results may differ from the reference program's by a relative error of at most 0.0055.
Values may be sent and summed in bfloat16 or wider, within the bound.
A program may use at most 32 MiB of HBM per device.

```python
import math
import jax
import jax.numpy as jnp
import numpy as np
from jax import lax

D = 4096
FF = 1024
TOP = 8
TOKENS = 1024
EXPERTS = 128
CAP = 160


def levels(rng, extent, split, least, largest):
    factor_of, own = 1.0, jax.random.fold_in(rng, 6)
    for axis_at, blocks in split:
        steps = jnp.exp(jax.random.uniform(jax.random.fold_in(own, axis_at), (blocks,), jnp.float32, least / len(split), largest / len(split)))
        factor_of = factor_of * jnp.repeat(steps, extent[axis_at] // blocks).reshape([-1 if axis == axis_at else 1 for axis in range(len(extent))])
    return factor_of


def deal_out(rng, own, number, rows, amount, top, reach, lean):
    order = jax.random.permutation(rng, amount)
    crowded, common = load_shares(amount, rows * top, reach, lean, True), load_shares(amount, rows * top, reach, lean, False)
    places = jnp.arange(amount)

    def named(sizes, turn):
        used = int((sizes > 0).sum())
        fixed = max(1, used // 4)
        passed = fixed + (places - fixed + turn * (used - fixed)) % max(1, amount - fixed)
        return jnp.zeros((amount,), jnp.int32).at[order[jnp.where(places < fixed, places, passed)]].set(jnp.asarray(sizes, jnp.int32))

    sizes = jnp.where(number % 4 == 0, named(crowded, number // 4), named(common, number - number // 4 - 1))
    mixed = jax.random.permutation(jax.random.fold_in(own, 3), amount)
    donor, sink = mixed[0:amount // 2 * 2:2], mixed[1:amount // 2 * 2:2]
    slack = jnp.minimum(sizes[donor] - 1, reach - sizes[sink]) // 2
    slack = jnp.where((donor == order[0]) | (sink == order[0]) | (sizes[sink] == 0), 0, jnp.maximum(slack, 0))
    passed = jax.random.randint(jax.random.fold_in(own, 4), (amount // 2,), 0, 1 << 20) % (slack + 1)
    sizes = sizes.at[donor].add(-passed).at[sink].add(passed)
    labels = jnp.searchsorted(jnp.cumsum(sizes), jnp.arange(rows * top), side="right").astype(jnp.int32)
    grid = labels.reshape(top, rows).T
    grid = grid[jax.random.permutation(jax.random.fold_in(own, 1), rows)]
    turn = jax.random.randint(jax.random.fold_in(own, 2), (rows, 1), 0, top)
    return jnp.take_along_axis(grid, (jnp.arange(top)[None, :] + turn) % top, axis=1)


def load_shares(amount, total, reach, slope, full):
    weights = [(1 << 20) // math.isqrt(grade ** slope) + 1 for grade in range(1, amount + 1)]
    largest = reach if full else min(reach, max(-(-total // amount), total * weights[0] // sum(weights)))
    least = 1 if total - largest >= amount - 1 else 0
    holding, surplus = [largest] + [least] * (amount - 1), total - largest - least * (amount - 1)
    while surplus > 0:
        free = [i for i in range(1, amount) if holding[i] < largest] or [i for i in range(1, amount) if holding[i] < reach]
        mass, remaining = sum([weights[i] for i in free]), surplus
        for i in free:
            more = min(reach - holding[i], max(1, remaining * weights[i] // mass), surplus)
            holding[i] = holding[i] + more
            surplus = surplus - more
    return np.array(holding)


def bell_draw(own_key, extent, spread, reach, pieces=(), held_as=jnp.bfloat16):
    drawn = spread * jax.random.normal(own_key, extent, jnp.float32)
    if pieces:
        drawn = drawn * levels(own_key, extent, pieces, -0.22, 0.18)
    return jnp.clip(drawn, -reach, reach).astype(held_as)


def setup_inputs(seed: int = 0) -> dict:
    seeds = jax.random.split(jax.random.key(seed), 8)
    tokens = bell_draw(seeds[0], (TOKENS, D), 1.0, 6.0, ((0, 128), (1, 8)))
    expert_ids_keys = jax.random.split(jax.random.fold_in(seeds[1], 1), TOKENS // TOKENS)
    expert_ids_turns = jax.random.permutation(jax.random.fold_in(seeds[1], 3), TOKENS // TOKENS)
    expert_ids = jax.vmap(lambda own, number: deal_out(jax.random.fold_in(seeds[1], 2), own, number, TOKENS, EXPERTS, TOP, CAP, 2))(expert_ids_keys, expert_ids_turns).reshape((TOKENS, TOP))
    route_weight = jnp.clip(jnp.exp(jax.random.uniform(seeds[2], (TOKENS, TOP), jnp.float32, math.log(0.1), math.log(1.0))), 0.1, 1.0)
    owner = jax.random.permutation(seeds[3], EXPERTS).astype(jnp.int32)
    gate_weight = bell_draw(seeds[4], (EXPERTS, D, FF), D ** -0.5, 0.09375, ((0, 128), (1, 8)))
    up_weight = bell_draw(seeds[5], (EXPERTS, D, FF), D ** -0.5, 0.09375, ((0, 128), (1, 8)))
    down_weight = bell_draw(seeds[6], (EXPERTS, FF, D), FF ** -0.5, 0.1875, ((0, 128), (2, 8)))
    return {"tokens": tokens, "expert_ids": expert_ids, "route_weight": route_weight, "owner": owner, "gate_weight": gate_weight, "up_weight": up_weight, "down_weight": down_weight}


def reference(tokens, expert_ids, route_weight, owner, gate_weight, up_weight, down_weight):
    def expert_step(total, expert):
        hit = expert_ids == expert
        taken = jnp.any(hit, axis=1)
        weight = jnp.sum(jnp.where(hit, route_weight, jnp.float32(0.0)), axis=1)
        order = jnp.argsort(jnp.where(taken, 0, 1).astype(jnp.int32), stable=True)
        picks = order[:CAP]
        valid = taken[picks]
        chosen = tokens[picks]
        slot = owner[expert]
        gate = jnp.dot(chosen, gate_weight[slot], preferred_element_type=jnp.float32)
        up = jnp.dot(chosen, up_weight[slot], preferred_element_type=jnp.float32)
        hidden = (jax.nn.silu(gate) * up).astype(jnp.bfloat16)
        output = jnp.dot(hidden, down_weight[slot], preferred_element_type=jnp.float32)
        scaled = output * jnp.where(valid, weight[picks], jnp.float32(0.0))[:, None]
        return total.at[picks].add(scaled), None

    start = jnp.zeros((TOKENS, D), jnp.float32)
    total, unused = lax.scan(expert_step, start, jnp.arange(EXPERTS, dtype=jnp.int32))
    return total.astype(jnp.bfloat16)
```

```python
import functools
import math

import jax
import jax.numpy as jnp
from jax import lax
from jax.experimental import pallas as pl
from jax.experimental.pallas import tpu as pltpu
from jax.sharding import PartitionSpec as P

BF16, F32, I32 = jnp.bfloat16, jnp.float32, jnp.int32
MESH = pl.DeviceIdType.MESH


def kernel(n, zhi, cap, ids_ref, rw_ref, owner_ref, tok_ref, gate_ref, up_ref, down_ref, out_ref,
           w1, w2, zbuf, tok, sel, wcol, hid, psend, precv, zsend, zrecv, acc, rbuf, tot, fsend, frecv,
           yrecv,
           w_sem, d_sem, z_send, z_recv, f_send, f_recv, s_send, s_recv, c_send, c_recv, q_send, q_recv,
           h_send, h_recv, k_send, k_recv, r_send, r_recv, g_send, g_recv, y_send, y_recv):
    rows, feat = tok_ref.shape
    ff = down_ref.shape[1]
    half = ff // 2
    part = half // zhi
    pair = 2 * rows
    block = n * pair
    chunk = block // 2
    total_rows = n * block
    grp, tp = lax.axis_index("grp"), lax.axis_index("tp")
    x, zlo, y = lax.rem(grp, n), lax.rem(lax.div(grp, n), 2), lax.div(grp, 2 * n)
    zh, core = lax.div(tp, 2), lax.rem(tp, 2)
    f = x * (1 - core) + y * core
    s = y * (1 - core) + x * core

    def at(f_, s_, z_):
        y_ = s_ * (1 - core) + f_ * core
        x_ = f_ * (1 - core) + s_ * core
        return ((y_ * 2 + z_) * n + x_, tp)

    f_peer = [None] + [at(lax.rem(f + k, n), s, zlo) for k in range(1, n)]
    s_peer = {1: at(f, lax.rem(s + 1, n), zlo), -1: at(f, lax.rem(s + n - 1, n), zlo)}
    z_peer = at(f, s, 1 - zlo)
    sibling = (grp, zh * 2 + (1 - core))
    q_peer = [None] + [(grp, lax.rem(zh + j, zhi) * 2 + core) for j in range(1, zhi)]

    def send(src, dst, ssem, rsem, device):
        copy = pltpu.make_async_remote_copy(src_ref=src, dst_ref=dst, send_sem=ssem, recv_sem=rsem,
                                            device_id=device, device_id_type=MESH)
        copy.start()
        return copy

    def arrived(dst, ssem, rsem, device):
        pltpu.make_async_remote_copy(src_ref=dst, dst_ref=dst, send_sem=ssem, recv_sem=rsem,
                                     device_id=device, device_id_type=MESH).wait_recv()

    sent = []

    loads = []
    for slot in range(2):
        side = (1 - core) if slot == 0 else core
        for q in range(zhi):
            for m, ref in enumerate((gate_ref, up_ref)):
                column = pl.multiple_of(side * half + q * part, part)
                load = pltpu.make_async_copy(ref.at[0, :, pl.ds(column, part)],
                                             w1.at[slot, q, :, pl.ds(m * part, part)], w_sem.at[slot, q, m])
                load.start()
                loads.append(load)
    load_down = pltpu.make_async_copy(down_ref.at[0], w2, d_sem)
    load_down.start()

    peers = f_peer[1:] + [s_peer[1], s_peer[-1], z_peer, sibling] + q_peer[1:]
    barrier = pltpu.get_barrier_semaphore()
    for peer in peers:
        pl.semaphore_signal(barrier, inc=1, device_id=peer, device_id_type=MESH)
    pl.semaphore_wait(barrier, len(peers))

    mine8 = pl.ds(pl.multiple_of(zlo * rows, rows), rows)
    zbuf[mine8, :] = tok_ref[...].astype(F32)
    sent.append(send(zbuf.at[mine8], zbuf.at[mine8], z_send, z_recv, z_peer))
    arrived(zbuf.at[pl.ds(pl.multiple_of((1 - zlo) * rows, rows), rows)], z_send, z_recv, z_peer)

    def at16(s_, f_):
        return pl.ds(pl.multiple_of(s_ * block + f_ * pair, pair), pair)

    tok[at16(s, f), :] = zbuf[...].astype(BF16)
    for k in range(1, n):
        sent.append(send(tok.at[at16(s, f)], tok.at[at16(s, f)], f_send.at[k], f_recv.at[k], f_peer[k]))

    experts = owner_ref.shape[1]
    mine = jnp.sum(jnp.where(owner_ref[...] == grp, lax.broadcasted_iota(I32, (1, experts), 1), 0),
                   axis=1, keepdims=True)
    hit = ids_ref[...] == mine
    taken = jnp.max(jnp.where(hit, 1.0, 0.0), axis=0, keepdims=True)
    weight = jnp.sum(jnp.where(hit, rw_ref[...], 0.0), axis=0, keepdims=True)
    high = weight.astype(BF16).astype(F32)
    middle = (weight - high).astype(BF16).astype(F32)
    low = weight - high - middle
    line = lax.broadcasted_iota(I32, (8, total_rows), 0)
    packed = jnp.where(line == 0, taken, jnp.where(line == 1, high, jnp.where(line == 2, middle,
                       jnp.where(line == 3, low, 0.0)))).astype(BF16)
    place_at = lax.broadcasted_iota(I32, (1, total_rows), 1)
    bits = [int(math.log2(v)) for v in (rows, 2, n, n)]
    i_ = place_at & (rows - 1)
    z_ = lax.shift_right_logical(place_at, bits[0]) & 1
    f_ = lax.shift_right_logical(place_at, bits[0] + 1) & (n - 1)
    s_ = lax.shift_right_logical(place_at, bits[0] + 1 + bits[2])
    y_ = s_ * (1 - core) + f_ * core
    x_ = f_ * (1 - core) + s_ * core
    row_of = ((y_ * 2 + z_) * n + x_) * rows + i_
    moved = jnp.zeros((8, total_rows), F32)
    place = jnp.zeros((8, total_rows), F32)
    step = min(256, total_rows)
    for base in range(0, total_rows, step):
        row = lax.broadcasted_iota(I32, (step, total_rows), 0) + base
        left = packed[:, base:base + step]
        moved += jnp.dot(left, jnp.where(row == row_of, 1.0, 0.0).astype(BF16), preferred_element_type=F32)
        place += jnp.dot(left, jnp.where(row < row_of, 1.0, 0.0).astype(BF16), preferred_element_type=F32)
    taken_at, place_of = moved[0:1], place[0:1]
    weight_at = moved[1:2] + moved[2:3] + moved[3:4]
    slot_at = lax.broadcasted_iota(I32, (cap, block), 0).astype(F32)
    weights = jnp.zeros((cap, 1), F32)
    for t in range(n):
        here = slice(t * block, (t + 1) * block)
        one = jnp.where((place_of[:, here] == slot_at) & (taken_at[:, here] > 0.5), 1.0, 0.0)
        sel[t] = one.astype(BF16)
        weights += jnp.sum(one * weight_at[:, here], axis=1, keepdims=True)
    wcol[...] = jnp.broadcast_to(weights, wcol.shape)

    for k in range(1, n):
        arrived(tok.at[at16(s, lax.rem(f + n - k, n))], f_send.at[k], f_recv.at[k], f_peer[k])

    def at_chunk(s_, c):
        return pl.ds(pl.multiple_of(s_ * block + c * chunk, chunk), chunk)

    def hops(direction, c):
        return n // 2 if (direction > 0) == (c == 0) else n // 2 - 1

    ways = [(w, direction, c) for c in range(2) for w, direction in enumerate((1, -1))]
    for w, direction, c in ways:
        if hops(direction, c) > 0:
            sent.append(send(tok.at[at_chunk(s, c)], tok.at[at_chunk(s, c)],
                             s_send.at[w, c, 0], s_recv.at[w, c, 0], s_peer[direction]))

    def rows_of(t):
        return jnp.dot(sel[t], tok[pl.ds(pl.multiple_of(t * block, block), block), :],
                       preferred_element_type=F32)

    picked = rows_of(s)
    for h in range(1, n // 2 + 1):
        for w, direction, c in ways:
            if h > hops(direction, c):
                continue
            came = at_chunk(lax.rem(s + n - direction * h, n), c)
            arrived(tok.at[came], s_send.at[w, c, h - 1], s_recv.at[w, c, h - 1], s_peer[direction])
            if h + 1 <= hops(direction, c):
                sent.append(send(tok.at[came], tok.at[came],
                                 s_send.at[w, c, h], s_recv.at[w, c, h], s_peer[direction]))
        picked += rows_of(lax.rem(s + h, n))
        if h < n // 2:
            picked += rows_of(lax.rem(s + n - h, n))
    rows_x = picked.astype(BF16)

    for load in loads:
        load.wait()
    order = [1] if zhi == 2 else [2, 1, 3]
    order = order + [0]
    for j in order:
        q = lax.rem(zh + j, zhi)
        psend[j] = jnp.dot(rows_x, w1[0, q], preferred_element_type=F32)
        sent.append(send(psend.at[j], precv.at[j], c_send.at[j], c_recv.at[j], sibling))
    own = None
    for j in order:
        q = lax.rem(zh + j, zhi)
        product = jnp.dot(rows_x, w1[1, q], preferred_element_type=F32)
        arrived(precv.at[j], c_send.at[j], c_recv.at[j], sibling)
        both = product + precv[j]
        if j == 0:
            own = both
        else:
            zsend[j] = both.astype(BF16)
            sent.append(send(zsend.at[j], zrecv.at[j], q_send.at[j], q_recv.at[j], q_peer[j]))

    for j in range(1, zhi):
        arrived(zrecv.at[j], q_send.at[j], q_recv.at[j], q_peer[j])
        own += zrecv[j].astype(F32)
    gate, up = own[:, :part], own[:, part:]
    me = core * zhi + zh
    hid[me] = (gate / (1.0 + jnp.exp(-gate)) * up).astype(BF16)

    for j in order[:-1]:
        sent.append(send(hid.at[me], hid.at[me], h_send.at[j], h_recv.at[j], q_peer[j]))
    sent.append(send(hid.at[me], hid.at[me], k_send.at[0], k_recv.at[0], sibling))
    load_down.wait()
    for j in order[:-1][::-1]:
        came = core * zhi + lax.rem(zh + zhi - j, zhi)
        arrived(hid.at[came], h_send.at[j], h_recv.at[j], q_peer[j])
        sent.append(send(hid.at[came], hid.at[came], k_send.at[j], k_recv.at[j], sibling))
    for j in range(zhi):
        came = (1 - core) * zhi + lax.rem(zh + zhi - j, zhi)
        arrived(hid.at[came], k_send.at[j], k_recv.at[j], sibling)

    hidden = jnp.concatenate([hid[m] for m in range(2 * zhi)], axis=1)
    result = jnp.dot(hidden, w2[...], preferred_element_type=F32)
    result = (result * wcol[:, 0:1]).astype(BF16)

    def spread(t):
        acc[pl.ds(pl.multiple_of(t * block, block), block), :] = lax.dot_general(
            sel[t], result, (((0,), (0,)), ((), ())), preferred_element_type=F32).astype(BF16)

    def pass_on(w, direction, c, k):
        length = hops(direction, c)
        to = lax.rem(s + 2 * n + direction * (length - k), n)
        if k > 0:
            arrived(rbuf.at[w, c, k - 1], r_send.at[w, c, k - 1], r_recv.at[w, c, k - 1], s_peer[direction])
            acc[at_chunk(to, c), :] = (acc[at_chunk(to, c), :].astype(F32) + rbuf[w, c, k - 1].astype(F32)).astype(BF16)
        sent.append(send(acc.at[at_chunk(to, c)], rbuf.at[w, c, k], r_send.at[w, c, k], r_recv.at[w, c, k],
                         s_peer[direction]))

    spread(lax.rem(s + n // 2, n))
    for w, direction, c in ways:
        if hops(direction, c) == n // 2:
            pass_on(w, direction, c, 0)
    for h in range(n // 2 - 1, 0, -1):
        spread(lax.rem(s + h, n))
        spread(lax.rem(s + n - h, n))
        if h == n // 2 - 1:
            for w, direction, c in ways:
                if hops(direction, c) == h:
                    pass_on(w, direction, c, 0)
    spread(s)
    for k in range(1, n // 2):
        for w, direction, c in ways:
            if k < hops(direction, c):
                pass_on(w, direction, c, k)
    for c in range(2):
        summed = acc[at_chunk(s, c), :].astype(F32)
        for w, direction in enumerate((1, -1)):
            k = hops(direction, c) - 1
            if k >= 0:
                arrived(rbuf.at[w, c, k], r_send.at[w, c, k], r_recv.at[w, c, k], s_peer[direction])
                summed += rbuf[w, c, k].astype(F32)
        tot[c * chunk:(c + 1) * chunk, :] = summed
        fsend[c * chunk:(c + 1) * chunk, :] = summed.astype(BF16)

    def at_pair(f_):
        return pl.ds(pl.multiple_of(f_ * pair, pair), pair)

    for k in range(1, n):
        to = at_pair(lax.rem(f + k, n))
        sent.append(send(fsend.at[to], frecv.at[k], g_send.at[k], g_recv.at[k], f_peer[k]))
    summed = tot[at_pair(f), :]
    for k in range(1, n):
        arrived(frecv.at[k], g_send.at[k], g_recv.at[k], f_peer[k])
        summed += frecv[k].astype(F32)
    zbuf2 = yrecv
    zbuf2[0:pair, :] = summed
    theirs = pl.ds(pl.multiple_of((1 - zlo) * rows, rows), rows)
    sent.append(send(zbuf2.at[theirs], zbuf2.at[pl.ds(pair, rows)], y_send, y_recv, z_peer))
    arrived(zbuf2.at[pl.ds(pair, rows)], y_send, y_recv, z_peer)
    out_ref[...] = (zbuf2[mine8, :] + zbuf2[pair:pair + rows, :]).astype(out_ref.dtype)

    for copy in sent:
        copy.wait_send()


def on_device(n, zhi, tokens, expert_ids, route_weight, owner, gate_weight, up_weight, down_weight):
    rows, feat = tokens.shape
    total_rows = expert_ids.shape[0]
    ff = gate_weight.shape[2]
    part = ff // 2 // zhi
    cap = min(20 * rows, total_rows)
    pair = 2 * rows
    block = n * pair
    chunk = block // 2
    half_ring = max(n // 2, 1)
    dma = pltpu.SemaphoreType.DMA
    vmem = pl.BlockSpec(memory_space=pltpu.VMEM)
    hbm = pl.BlockSpec(memory_space=pl.ANY)
    return pl.pallas_call(
        functools.partial(kernel, n, zhi, cap),
        out_shape=jax.ShapeDtypeStruct((rows, feat), BF16),
        in_specs=[vmem] * 4 + [hbm] * 3,
        out_specs=vmem,
        scratch_shapes=[
            pltpu.VMEM((2, zhi, feat, 2 * part), BF16),
            pltpu.VMEM((ff, feat), BF16),
            pltpu.VMEM((pair, feat), F32),
            pltpu.VMEM((total_rows, feat), BF16),
            pltpu.VMEM((n, cap, block), BF16),
            pltpu.VMEM((cap, 128), F32),
            pltpu.VMEM((2 * zhi, cap, part), BF16),
            pltpu.VMEM((zhi, cap, 2 * part), F32),
            pltpu.VMEM((zhi, cap, 2 * part), F32),
            pltpu.VMEM((zhi, cap, 2 * part), BF16),
            pltpu.VMEM((zhi, cap, 2 * part), BF16),
            pltpu.VMEM((total_rows, feat), BF16),
            pltpu.VMEM((2, 2, half_ring, chunk, feat), BF16),
            pltpu.VMEM((block, feat), F32),
            pltpu.VMEM((block, feat), BF16),
            pltpu.VMEM((n, pair, feat), BF16),
            pltpu.VMEM((pair + rows, feat), F32),
            dma((2, zhi, 2)), dma,
            dma, dma,
            dma((n,)), dma((n,)),
            dma((2, 2, half_ring)), dma((2, 2, half_ring)),
            dma((zhi,)), dma((zhi,)),
            dma((zhi,)), dma((zhi,)),
            dma((zhi,)), dma((zhi,)),
            dma((zhi,)), dma((zhi,)),
            dma((2, 2, half_ring)), dma((2, 2, half_ring)),
            dma((n,)), dma((n,)),
            dma, dma,
        ],
        compiler_params=pltpu.CompilerParams(
            collective_id=0, has_side_effects=True, vmem_limit_bytes=40 * 1024 * 1024
        ),
        cost_estimate=pl.CostEstimate(flops=2 * cap * feat * ff * 3, bytes_accessed=6 * feat * ff,
                                      transcendentals=cap * ff // 8),
    )(expert_ids.T, route_weight.T, owner.reshape(1, -1), tokens, gate_weight, up_weight, down_weight)


def solution(mesh):
    n = math.isqrt(mesh.shape["grp"] // 2)
    return jax.shard_map(
        functools.partial(on_device, n, mesh.shape["tp"] // 2),
        mesh=mesh,
        in_specs=(
            P("grp", "tp"),
            P(),
            P(),
            P(),
            P("grp", "tp", None),
            P("grp", "tp", None),
            P("grp", None, "tp"),
        ),
        out_specs=P("grp", "tp"),
        check_vma=False,
    )
```

```python
import functools
import math

import jax
import jax.numpy as jnp
from jax import lax
from jax.experimental import pallas as pl
from jax.experimental.pallas import tpu as pltpu
from jax.sharding import PartitionSpec as P

BF16, F32, I32 = jnp.bfloat16, jnp.float32, jnp.int32
MESH = pl.DeviceIdType.MESH


TREE = "two"


def parents(tree, length):
    if tree == "ring":
        return {d: d - 1 for d in range(1, length + 1)}
    if tree == "direct":
        return {d: 0 for d in range(1, length + 1)}
    return {d: 0 if d <= 2 else 2 for d in range(1, length + 1)}


def kernel(n, zhi, cap, tree, ids_hbm, rw_hbm, owner_hbm, tok_hbm, gate_ref, up_ref, down_ref, out_ref,
           ids_ref, rw_ref, owner_ref, tok_ref, w1, w2, stage, tok, sel, sel_t, wcol, hid, psend, precv, zsend, zrecv, acc, rbuf, tot, fsend, frecv,
           i_sem, w_sem, d_sem, f_send, f_recv, s_send, s_recv, c_send, c_recv, q_send, q_recv,
           h_send, h_recv, k_send, k_recv, r_send, r_recv, g_send, g_recv):
    rows, feat = tok_ref.shape
    ff = down_ref.shape[1]
    half = ff // 2
    part = half // zhi
    pair = 2 * rows
    block = n * pair
    chunk = block // 2
    total_rows = n * block
    grp, tp = lax.axis_index("grp"), lax.axis_index("tp")
    x, zlo, y = lax.rem(grp, n), lax.rem(lax.div(grp, n), 2), lax.div(grp, 2 * n)
    zh, core = lax.div(tp, 2), lax.rem(tp, 2)
    f = x * (1 - core) + y * core
    s = y * (1 - core) + x * core

    def at(f_, s_, z_):
        y_ = s_ * (1 - core) + f_ * core
        x_ = f_ * (1 - core) + s_ * core
        return ((y_ * 2 + z_) * n + x_, tp)

    def other_z(dz):
        return zlo + dz - 2 * zlo * dz

    near = [(k, dz) for k in range(n) for dz in range(2)][1:]
    f_peer = {(k, dz): at(lax.rem(f + k, n), s, other_z(dz)) for k, dz in near}
    ways = [(w, direction, c) for c in range(2) for w, direction in enumerate((1, -1))]

    def hops(direction, c):
        return n // 2 if (direction > 0) == (c == 0) else n // 2 - 1

    def from_(direction, c):
        return parents(tree, hops(direction, c))

    steps = sorted({d - p for w, direction, c in ways for d, p in from_(direction, c).items()})
    s_peer = {sign * d: at(f, lax.rem(s + n + sign * d, n), zlo) for d in steps for sign in (1, -1)}
    if 2 * max(steps) == n:
        del s_peer[-max(steps)]

    def s_to(d):
        return s_peer[d] if d in s_peer else s_peer[-d]

    sibling = (grp, zh * 2 + (1 - core))
    q_peer = [None] + [(grp, lax.rem(zh + j, zhi) * 2 + core) for j in range(1, zhi)]

    def send(src, dst, ssem, rsem, device):
        copy = pltpu.make_async_remote_copy(src_ref=src, dst_ref=dst, send_sem=ssem, recv_sem=rsem,
                                            device_id=device, device_id_type=MESH)
        copy.start()
        return copy

    def arrived(dst, ssem, rsem, device):
        pltpu.make_async_remote_copy(src_ref=dst, dst_ref=dst, send_sem=ssem, recv_sem=rsem,
                                     device_id=device, device_id_type=MESH).wait_recv()

    sent = []

    peers = list(f_peer.values()) + list(s_peer.values()) + [sibling] + q_peer[1:]
    barrier = pltpu.get_barrier_semaphore()
    for peer in peers:
        pl.semaphore_signal(barrier, inc=1, device_id=peer, device_id_type=MESH)

    small = []
    for m, (src, dst) in enumerate(((tok_hbm, tok_ref), (ids_hbm, ids_ref), (rw_hbm, rw_ref), (owner_hbm, owner_ref))):
        load = pltpu.make_async_copy(src, dst, i_sem.at[m])
        load.start()
        small.append(load)

    loads = []
    for slot in range(2):
        side = (1 - core) if slot == 0 else core
        for q in range(zhi):
            for m, ref in enumerate((gate_ref, up_ref)):
                column = pl.multiple_of(side * half + q * part, part)
                load = pltpu.make_async_copy(ref.at[0, :, pl.ds(column, part)],
                                             w1.at[slot, q, :, pl.ds(m * part, part)], w_sem.at[slot, q, m])
                load.start()
                loads.append(load)
    load_down = pltpu.make_async_copy(down_ref.at[0], w2, d_sem)
    load_down.start()

    for load in small:
        load.wait()
    pl.semaphore_wait(barrier, len(peers))

    def fold(v):
        return jnp.concatenate([v[..., :feat // 2], v[..., feat // 2:]], axis=-2)

    def unfold(v):
        return jnp.concatenate([v[..., :rows, :], v[..., rows:, :]], axis=-1)

    mine2 = f * 2 + zlo
    stage[mine2] = fold(tok_ref[...].astype(F32)).astype(BF16)
    for m, (k, dz) in enumerate(near):
        sent.append(send(stage.at[mine2], stage.at[mine2], f_send.at[m], f_recv.at[m], f_peer[k, dz]))

    experts = owner_ref.shape[1]
    mine = jnp.sum(jnp.where(owner_ref[...] == grp, lax.broadcasted_iota(I32, (1, experts), 1), 0),
                   axis=1, keepdims=True)
    hit = ids_ref[...] == mine
    taken = jnp.max(jnp.where(hit, 1.0, 0.0), axis=0, keepdims=True)
    weight = jnp.sum(jnp.where(hit, rw_ref[...], 0.0), axis=0, keepdims=True)
    high = weight.astype(BF16).astype(F32)
    middle = (weight - high).astype(BF16).astype(F32)
    low = weight - high - middle
    lanes = block

    def square(v):
        wide = jnp.broadcast_to(v, (n, total_rows))
        at_row = lax.broadcasted_iota(I32, (n, lanes), 0)
        return sum(jnp.where(at_row == a, wide[:, a * lanes:(a + 1) * lanes], 0.0) for a in range(n))

    taken_sq = square(taken)
    before = jnp.where(lax.broadcasted_iota(I32, (lanes, lanes), 0) < lax.broadcasted_iota(I32, (lanes, lanes), 1),
                       1.0, 0.0).astype(BF16)
    in_line = jnp.dot(taken_sq.astype(BF16), before, preferred_element_type=F32)
    counts = jnp.sum(taken_sq, axis=1, keepdims=True)
    ahead = jnp.zeros((n, lanes), F32)
    at_row = lax.broadcasted_iota(I32, (n, lanes), 0)
    for a in range(n - 1):
        ahead += jnp.where(at_row > a, counts[a:a + 1, :], 0.0)
    place_sq = jnp.where(taken_sq > 0.5, in_line + ahead, -1.0)
    stacked = jnp.concatenate([place_sq, square(high), square(middle), square(low)], axis=0).astype(BF16)
    position = lax.broadcasted_iota(I32, (1, total_rows), 1)
    bits = [int(math.log2(v)) for v in (rows, n)]
    i_ = position & (rows - 1)
    z_ = lax.shift_right_logical(position, bits[0]) & 1
    f_ = lax.shift_right_logical(position, bits[0] + 1) & (n - 1)
    s_ = lax.shift_right_logical(position, bits[0] + 1 + bits[1])
    y_ = s_ * (1 - core) + f_ * core
    x_ = f_ * (1 - core) + s_ * core
    lane_of = (z_ * n + x_) * rows + i_
    take = jnp.where(lax.broadcasted_iota(I32, (lanes, total_rows), 0) == lane_of, 1.0, 0.0).astype(BF16)
    spread_out = jnp.dot(stacked, take, preferred_element_type=F32)
    keep = lax.broadcasted_iota(I32, (n, total_rows), 0) == y_

    def line(m):
        return jnp.sum(jnp.where(keep, spread_out[m * n:(m + 1) * n], 0.0), axis=0, keepdims=True)

    place_of = line(0)
    weight_at = line(1) + line(2) + line(3)
    slot_at = lax.broadcasted_iota(I32, (cap, block), 0).astype(F32)
    weights = jnp.zeros((cap, block), F32)
    for t in range(n):
        here = slice(t * block, (t + 1) * block)
        one = jnp.where(place_of[:, here] == slot_at, 1.0, 0.0)
        sel[t] = one.astype(BF16)
        weights += one * weight_at[:, here]
    wcol[...] = jnp.broadcast_to(jnp.sum(weights, axis=1, keepdims=True), wcol.shape)

    for m, (k, dz) in enumerate(near):
        came = lax.rem(f + n - k, n) * 2 + other_z(dz)
        arrived(stage.at[came], f_send.at[m], f_recv.at[m], f_peer[k, dz])
    tok[pl.ds(pl.multiple_of(s * block, block), block), :] = (
        unfold(stage[...].astype(F32)).reshape(block, feat).astype(BF16))

    def at_chunk(s_, c):
        return pl.ds(pl.multiple_of(s_ * block + c * chunk, chunk), chunk)

    order_out = sorted(range(1, n // 2 + 1), key=lambda d: (d not in parents(tree, n // 2).values(), -d))

    def hand_out(d, those):
        for e in order_out:
            for w, direction, c in those:
                if from_(direction, c).get(e) == d:
                    held = at_chunk(lax.rem(s + n - direction * d, n), c)
                    sent.append(send(tok.at[held], tok.at[held], s_send.at[w, c, e - 1], s_recv.at[w, c, e - 1],
                                     s_to(direction * (e - d))))

    hand_out(0, ways)

    def rows_of(*ts):
        return jnp.dot(jnp.concatenate([sel[t] for t in ts], axis=1),
                       jnp.concatenate([tok[pl.ds(pl.multiple_of(t * block, block), block), :] for t in ts], axis=0),
                       preferred_element_type=F32)

    picked = None
    for h in sorted(range(1, n // 2 + 1), key=lambda d: (d not in parents(tree, n // 2).values(), d)):
        for w, direction, c in ways:
            if h <= hops(direction, c):
                came = at_chunk(lax.rem(s + n - direction * h, n), c)
                arrived(tok.at[came], s_send.at[w, c, h - 1], s_recv.at[w, c, h - 1], s_to(direction))
                hand_out(h, [(w, direction, c)])
        more = rows_of(lax.rem(s + h, n), s if h == n // 2 else lax.rem(s + n - h, n))
        picked = more if picked is None else picked + more
    rows_x = picked.astype(BF16)

    for load in loads:
        load.wait()
    order = [1] if zhi == 2 else [2, 1, 3]
    order = order + [0]

    def for_sibling(j):
        psend[j] = jnp.dot(rows_x, w1[0, lax.rem(zh + j, zhi)], preferred_element_type=F32)
        sent.append(send(psend.at[j], precv.at[j], c_send.at[j], c_recv.at[j], sibling))

    own = None
    for_sibling(order[0])
    for m, j in enumerate(order):
        if m + 1 < zhi:
            for_sibling(order[m + 1])
        product = jnp.dot(rows_x, w1[1, lax.rem(zh + j, zhi)], preferred_element_type=F32)
        arrived(precv.at[j], c_send.at[j], c_recv.at[j], sibling)
        both = product + precv[j]
        if j == 0:
            own = both
        else:
            zsend[j] = both.astype(BF16)
            sent.append(send(zsend.at[j], zrecv.at[j], q_send.at[j], q_recv.at[j], q_peer[j]))

    for t in range(n):
        sel_t[t] = sel[t].astype(F32).T.astype(BF16)
    load_down.wait()
    for j in order[:-1][::-1]:
        arrived(zrecv.at[j], q_send.at[j], q_recv.at[j], q_peer[j])
        own += zrecv[j].astype(F32)
    gate, up = own[:, :part], own[:, part:]
    me = core * zhi + zh
    hid[me] = (gate / (1.0 + jnp.exp(-gate)) * up).astype(BF16)

    for j in order[:-1]:
        sent.append(send(hid.at[me], hid.at[me], h_send.at[j], h_recv.at[j], q_peer[j]))
    sent.append(send(hid.at[me], hid.at[me], k_send.at[0], k_recv.at[0], sibling))

    def down(*ms):
        return jnp.dot(jnp.concatenate([hid[m] for m in ms], axis=1),
                       jnp.concatenate([w2[pl.ds(pl.multiple_of(m * part, part), part), :] for m in ms], axis=0),
                       preferred_element_type=F32)

    theirs = (1 - core) * zhi
    for j in order[:-1][::-1]:
        came = core * zhi + lax.rem(zh + zhi - j, zhi)
        arrived(hid.at[came], h_send.at[j], h_recv.at[j], q_peer[j])
        sent.append(send(hid.at[came], hid.at[came], k_send.at[j], k_recv.at[j], sibling))
    result = None
    for j in order[::-1]:
        q = lax.rem(zh + zhi - j, zhi)
        arrived(hid.at[theirs + q], k_send.at[j], k_recv.at[j], sibling)
        more = down(core * zhi + q, theirs + q)
        result = more if result is None else result + more
    result = (result * wcol[:, 0:1]).astype(BF16)

    def spread(t):
        acc[pl.ds(pl.multiple_of(t * block, block), block), :] = jnp.dot(
            sel_t[t], result, preferred_element_type=F32).astype(BF16)

    def take_in(w, direction, c, d, onto):
        for e, p in from_(direction, c).items():
            if p == d:
                arrived(rbuf.at[w, c, e - 1], r_send.at[w, c, e - 1], r_recv.at[w, c, e - 1], s_to(direction))
                onto += rbuf[w, c, e - 1].astype(F32)
        return onto

    def pass_on(w, direction, c, d):
        of = at_chunk(lax.rem(s + n - direction * d, n), c)
        p = from_(direction, c)[d]
        if d in from_(direction, c).values():
            acc[of, :] = take_in(w, direction, c, d, acc[of, :].astype(F32)).astype(BF16)
        sent.append(send(acc.at[of], rbuf.at[w, c, d - 1], r_send.at[w, c, d - 1], r_recv.at[w, c, d - 1],
                         s_to(-direction * (d - p))))

    for d in range(n // 2, 0, -1):
        spread(lax.rem(s + d, n))
        if d < n // 2:
            spread(lax.rem(s + n - d, n))
        for w, direction, c in ways:
            if d <= hops(direction, c) and d not in from_(direction, c).values():
                pass_on(w, direction, c, d)
    spread(s)
    for d in range(n // 2, 0, -1):
        for w, direction, c in ways:
            if d <= hops(direction, c) and d in from_(direction, c).values():
                pass_on(w, direction, c, d)
    for c in range(2):
        summed = acc[at_chunk(s, c), :].astype(F32)
        for w, direction in enumerate((1, -1)):
            summed = take_in(w, direction, c, 0, summed)
        tot[c * chunk:(c + 1) * chunk, :] = summed

    fsend[...] = fold(tot[...].reshape(2 * n, rows, feat)).astype(BF16)
    for m, (k, dz) in enumerate(near):
        to = lax.rem(f + k, n) * 2 + other_z(dz)
        sent.append(send(fsend.at[to], frecv.at[m], g_send.at[m], g_recv.at[m], f_peer[k, dz]))
    summed = jnp.zeros((2 * rows, feat // 2), F32)
    for m, (k, dz) in enumerate(near):
        arrived(frecv.at[m], g_send.at[m], g_recv.at[m], f_peer[k, dz])
        summed += frecv[m].astype(F32)
    own8 = tot[pl.ds(pl.multiple_of(mine2 * rows, rows), rows), :]
    out_ref[...] = (own8 + unfold(summed)).astype(out_ref.dtype)

    for copy in sent:
        copy.wait_send()


def on_device(n, zhi, tokens, expert_ids, route_weight, owner, gate_weight, up_weight, down_weight):
    rows, feat = tokens.shape
    total_rows = expert_ids.shape[0]
    ff = gate_weight.shape[2]
    part = ff // 2 // zhi
    cap = min(20 * rows, total_rows)
    pair = 2 * rows
    block = n * pair
    chunk = block // 2
    half_ring = max(n // 2, 1)
    dma = pltpu.SemaphoreType.DMA
    vmem = pl.BlockSpec(memory_space=pltpu.VMEM)
    hbm = pl.BlockSpec(memory_space=pl.ANY)
    return pl.pallas_call(
        functools.partial(kernel, n, zhi, cap, TREE),
        out_shape=jax.ShapeDtypeStruct((rows, feat), BF16),
        in_specs=[hbm] * 7,
        out_specs=vmem,
        scratch_shapes=[
            pltpu.VMEM(expert_ids.shape[::-1], I32),
            pltpu.VMEM(route_weight.shape[::-1], F32),
            pltpu.VMEM((1, owner.shape[0]), I32),
            pltpu.VMEM((rows, feat), BF16),
            pltpu.VMEM((2, zhi, feat, 2 * part), BF16),
            pltpu.VMEM((ff, feat), BF16),
            pltpu.VMEM((2 * n, pair, feat // 2), BF16),
            pltpu.VMEM((total_rows, feat), BF16),
            pltpu.VMEM((n, cap, block), BF16),
            pltpu.VMEM((n, block, cap), BF16),
            pltpu.VMEM((cap, 128), F32),
            pltpu.VMEM((2 * zhi, cap, part), BF16),
            pltpu.VMEM((zhi, cap, 2 * part), F32),
            pltpu.VMEM((zhi, cap, 2 * part), F32),
            pltpu.VMEM((zhi, cap, 2 * part), BF16),
            pltpu.VMEM((zhi, cap, 2 * part), BF16),
            pltpu.VMEM((total_rows, feat), BF16),
            pltpu.VMEM((2, 2, half_ring, chunk, feat), BF16),
            pltpu.VMEM((block, feat), F32),
            pltpu.VMEM((2 * n, pair, feat // 2), BF16),
            pltpu.VMEM((2 * n - 1, pair, feat // 2), BF16),
            dma((4,)), dma((2, zhi, 2)), dma,
            dma((2 * n - 1,)), dma((2 * n - 1,)),
            dma((2, 2, half_ring)), dma((2, 2, half_ring)),
            dma((zhi,)), dma((zhi,)),
            dma((zhi,)), dma((zhi,)),
            dma((zhi,)), dma((zhi,)),
            dma((zhi,)), dma((zhi,)),
            dma((2, 2, half_ring)), dma((2, 2, half_ring)),
            dma((2 * n - 1,)), dma((2 * n - 1,)),
        ],
        compiler_params=pltpu.CompilerParams(
            collective_id=0, has_side_effects=True, vmem_limit_bytes=60 * 1024 * 1024
        ),
        cost_estimate=pl.CostEstimate(flops=2 * cap * feat * ff * 3, bytes_accessed=6 * feat * ff,
                                      transcendentals=cap * ff // 8),
    )(expert_ids.T, route_weight.T, owner.reshape(1, -1), tokens, gate_weight, up_weight, down_weight)


def solution(mesh):
    n = math.isqrt(mesh.shape["grp"] // 2)
    return jax.shard_map(
        functools.partial(on_device, n, mesh.shape["tp"] // 2),
        mesh=mesh,
        in_specs=(
            P("grp", "tp"),
            P(),
            P(),
            P(),
            P("grp", "tp", None),
            P("grp", "tp", None),
            P("grp", None, "tp"),
        ),
        out_specs=P("grp", "tp"),
        check_vma=False,
    )
```

```python
import functools
import math

import jax
import jax.numpy as jnp
from jax import lax
from jax.experimental import pallas as pl
from jax.experimental.pallas import tpu as pltpu
from jax.sharding import PartitionSpec as P

BF16, F32, I32 = jnp.bfloat16, jnp.float32, jnp.int32
MESH = pl.DeviceIdType.MESH


TREE = "two"
CHUNKS = 4


def parents(tree, length):
    if tree == "ring":
        return {d: d - 1 for d in range(1, length + 1)}
    if tree == "direct":
        return {d: 0 for d in range(1, length + 1)}
    return {d: 0 if d <= 2 else 2 for d in range(1, length + 1)}


def kernel(n, zhi, cap, tree, ids_hbm, rw_hbm, owner_hbm, tok_hbm, gate_ref, up_ref, down_ref, out_ref,
           ids_ref, rw_ref, owner_ref, tok_ref, w1, w2, stage, tok, sel, sel_t, wcol, hid, psend, precv, zsend, zrecv, acc, rbuf, tot, fsend, frecv,
           i_sem, w_sem, d_sem, f_send, f_recv, s_send, s_recv, c_send, c_recv, q_send, q_recv,
           h_send, h_recv, k_send, k_recv, r_send, r_recv, g_send, g_recv):
    rows, feat = tok_ref.shape
    ff = down_ref.shape[1]
    half = ff // 2
    part = half // zhi
    pair = 2 * rows
    block = n * pair
    chunk = block // CHUNKS
    total_rows = n * block
    grp, tp = lax.axis_index("grp"), lax.axis_index("tp")
    x, zlo, y = lax.rem(grp, n), lax.rem(lax.div(grp, n), 2), lax.div(grp, 2 * n)
    zh, core = lax.div(tp, 2), lax.rem(tp, 2)
    turn = core
    f = x * (1 - turn) + y * turn
    s = y * (1 - turn) + x * turn

    def at(f_, s_, z_):
        y_ = s_ * (1 - turn) + f_ * turn
        x_ = f_ * (1 - turn) + s_ * turn
        return ((y_ * 2 + z_) * n + x_, tp)

    def other_z(dz):
        return zlo + dz - 2 * zlo * dz

    near = sorted([(k, dz) for k in range(n) for dz in range(2)][1:], key=lambda v: -min(v[0], n - v[0]) - v[1])
    f_peer = {(k, dz): at(lax.rem(f + k, n), s, other_z(dz)) for k, dz in near}
    ways = [(w, direction, c) for c in range(CHUNKS) for w, direction in enumerate((1, -1))]

    def hops(direction, c):
        return n // 2 if (direction > 0) == (c % 2 == 0) else n // 2 - 1

    def from_(direction, c):
        return parents(tree, hops(direction, c))

    steps = sorted({d - p for w, direction, c in ways for d, p in from_(direction, c).items()})
    s_peer = {sign * d: at(f, lax.rem(s + n + sign * d, n), zlo) for d in steps for sign in (1, -1)}
    if 2 * max(steps) == n:
        del s_peer[-max(steps)]

    def s_to(d):
        return s_peer[d] if d in s_peer else s_peer[-d]

    sibling = (grp, zh * 2 + (1 - core))
    q_peer = [None] + [(grp, lax.rem(zh + j, zhi) * 2 + core) for j in range(1, zhi)]

    def send(src, dst, ssem, rsem, device):
        copy = pltpu.make_async_remote_copy(src_ref=src, dst_ref=dst, send_sem=ssem, recv_sem=rsem,
                                            device_id=device, device_id_type=MESH)
        copy.start()
        return copy

    def arrived(dst, ssem, rsem, device):
        pltpu.make_async_remote_copy(src_ref=dst, dst_ref=dst, send_sem=ssem, recv_sem=rsem,
                                     device_id=device, device_id_type=MESH).wait_recv()

    sent = []

    def load(src, dst, sem):
        copy = pltpu.make_async_copy(src, dst, sem)
        copy.start()
        return copy

    rows_in = load(tok_hbm, tok_ref, i_sem.at[0])
    peers = list(f_peer.values()) + list(s_peer.values()) + q_peer[1:] + [sibling]
    barrier = pltpu.get_barrier_semaphore()
    for peer in peers:
        pl.semaphore_signal(barrier, inc=1, device_id=peer, device_id_type=MESH)

    def fold(v):
        return jnp.concatenate([v[..., :feat // 2], v[..., feat // 2:]], axis=-2)

    def unfold(v):
        return jnp.concatenate([v[..., :rows, :], v[..., rows:, :]], axis=-1)

    mine2 = f * 2 + zlo
    rows_in.wait()
    stage[mine2] = fold(tok_ref[...].astype(F32)).astype(BF16)
    pl.semaphore_wait(barrier, len(peers))
    for m, (k, dz) in enumerate(near):
        sent.append(send(stage.at[mine2], stage.at[mine2], f_send.at[m], f_recv.at[m], f_peer[k, dz]))

    small = [load(ids_hbm, ids_ref, i_sem.at[1]), load(rw_hbm, rw_ref, i_sem.at[2]),
             load(owner_hbm, owner_ref, i_sem.at[3])]
    loads = [load(gate_ref.at[0], w1.at[0], w_sem.at[0]), load(up_ref.at[0], w1.at[1], w_sem.at[1])]
    load_down = load(down_ref.at[0], w2, d_sem)
    for copy in small:
        copy.wait()

    experts = owner_ref.shape[1]
    mine = jnp.sum(jnp.where(owner_ref[...] == grp, lax.broadcasted_iota(I32, (1, experts), 1), 0),
                   axis=1, keepdims=True)
    hit = ids_ref[...] == mine
    taken = jnp.max(jnp.where(hit, 1.0, 0.0), axis=0, keepdims=True)
    weight = jnp.sum(jnp.where(hit, rw_ref[...], 0.0), axis=0, keepdims=True)
    high = weight.astype(BF16).astype(F32)
    middle = (weight - high).astype(BF16).astype(F32)
    low = weight - high - middle
    lanes = block

    def square(v):
        wide = jnp.broadcast_to(v, (n, total_rows))
        at_row = lax.broadcasted_iota(I32, (n, lanes), 0)
        return sum(jnp.where(at_row == a, wide[:, a * lanes:(a + 1) * lanes], 0.0) for a in range(n))

    taken_sq = square(taken)
    before = jnp.where(lax.broadcasted_iota(I32, (lanes, lanes), 0) < lax.broadcasted_iota(I32, (lanes, lanes), 1),
                       1.0, 0.0).astype(BF16)
    in_line = jnp.dot(taken_sq.astype(BF16), before, preferred_element_type=F32)
    counts = jnp.sum(taken_sq, axis=1, keepdims=True)
    ahead = jnp.zeros((n, lanes), F32)
    at_row = lax.broadcasted_iota(I32, (n, lanes), 0)
    for a in range(n - 1):
        ahead += jnp.where(at_row > a, counts[a:a + 1, :], 0.0)
    place_sq = jnp.where(taken_sq > 0.5, in_line + ahead, -1.0)
    stacked = jnp.concatenate([place_sq, square(high), square(middle), square(low)], axis=0).astype(BF16)
    position = lax.broadcasted_iota(I32, (1, total_rows), 1)
    bits = [int(math.log2(v)) for v in (rows, n)]
    i_ = position & (rows - 1)
    z_ = lax.shift_right_logical(position, bits[0]) & 1
    f_ = lax.shift_right_logical(position, bits[0] + 1) & (n - 1)
    s_ = lax.shift_right_logical(position, bits[0] + 1 + bits[1])
    y_ = s_ * (1 - turn) + f_ * turn
    x_ = f_ * (1 - turn) + s_ * turn
    lane_of = (z_ * n + x_) * rows + i_
    take = jnp.where(lax.broadcasted_iota(I32, (lanes, total_rows), 0) == lane_of, 1.0, 0.0).astype(BF16)
    spread_out = jnp.dot(stacked, take, preferred_element_type=F32)
    keep = lax.broadcasted_iota(I32, (n, total_rows), 0) == y_

    def line(m):
        return jnp.sum(jnp.where(keep, spread_out[m * n:(m + 1) * n], 0.0), axis=0, keepdims=True)

    place_of = line(0)
    weight_at = line(1) + line(2) + line(3)
    slot_at = lax.broadcasted_iota(I32, (cap, block), 0).astype(F32)
    weights = jnp.zeros((cap, block), F32)
    for t in range(n):
        here = slice(t * block, (t + 1) * block)
        one = jnp.where(place_of[:, here] == slot_at, 1.0, 0.0)
        sel[t] = one.astype(BF16)
        weights += one * weight_at[:, here]
    wcol[...] = jnp.broadcast_to(jnp.sum(weights, axis=1, keepdims=True), wcol.shape)

    for m, (k, dz) in enumerate(near):
        came = lax.rem(f + n - k, n) * 2 + other_z(dz)
        arrived(stage.at[came], f_send.at[m], f_recv.at[m], f_peer[k, dz])
    tok[pl.ds(pl.multiple_of(s * block, block), block), :] = (
        unfold(stage[...].astype(F32)).reshape(block, feat).astype(BF16))

    def at_chunk(s_, c):
        return pl.ds(pl.multiple_of(s_ * block + c * chunk, chunk), chunk)

    order_out = sorted(range(1, n // 2 + 1), key=lambda d: (d not in parents(tree, n // 2).values(), -d))

    def hand_out(d, those):
        for e in order_out:
            for w, direction, c in those:
                if from_(direction, c).get(e) == d:
                    held = at_chunk(lax.rem(s + n - direction * d, n), c)
                    sent.append(send(tok.at[held], tok.at[held], s_send.at[w, c, e - 1], s_recv.at[w, c, e - 1],
                                     s_to(direction * (e - d))))

    hand_out(0, ways)

    def rows_of(*ts):
        return jnp.dot(jnp.concatenate([sel[t] for t in ts], axis=1),
                       jnp.concatenate([tok[pl.ds(pl.multiple_of(t * block, block), block), :] for t in ts], axis=0),
                       preferred_element_type=F32)

    picked = None
    for h in sorted(range(1, n // 2 + 1), key=lambda d: (d not in parents(tree, n // 2).values(), d)):
        for w, direction, c in ways:
            if h <= hops(direction, c):
                came = at_chunk(lax.rem(s + n - direction * h, n), c)
                arrived(tok.at[came], s_send.at[w, c, h - 1], s_recv.at[w, c, h - 1], s_to(direction))
                hand_out(h, [(w, direction, c)])
        more = rows_of(lax.rem(s + h, n), s if h == n // 2 else lax.rem(s + n - h, n))
        picked = more if picked is None else picked + more
    rows_x = picked.astype(BF16)

    for copy in loads:
        copy.wait()
    order = [1] if zhi == 2 else [2, 1, 3]
    order = order + [0]

    def partial(side, j):
        columns = pl.ds(pl.multiple_of(side * half + lax.rem(zh + j, zhi) * part, part), part)
        return jnp.dot(rows_x, jnp.concatenate([w1[0, :, columns], w1[1, :, columns]], axis=1),
                       preferred_element_type=F32)

    def for_sibling(j):
        psend[j] = partial(1 - core, j)
        sent.append(send(psend.at[j], precv.at[j], c_send.at[j], c_recv.at[j], sibling))

    own = None
    for_sibling(order[0])
    for m, j in enumerate(order):
        if m + 1 < zhi:
            for_sibling(order[m + 1])
        product = partial(core, j)
        arrived(precv.at[j], c_send.at[j], c_recv.at[j], sibling)
        both = product + precv[j]
        if j == 0:
            own = both
        else:
            zsend[j] = both.astype(BF16)
            sent.append(send(zsend.at[j], zrecv.at[j], q_send.at[j], q_recv.at[j], q_peer[j]))

    for t in range(n):
        sel_t[t] = sel[t].astype(F32).T.astype(BF16)
    load_down.wait()
    for j in order[:-1][::-1]:
        arrived(zrecv.at[j], q_send.at[j], q_recv.at[j], q_peer[j])
        own += zrecv[j].astype(F32)
    gate, up = own[:, :part], own[:, part:]
    me = core * zhi + zh
    hid[me] = (gate / (1.0 + jnp.exp(-gate)) * up).astype(BF16)

    for j in order[:-1]:
        sent.append(send(hid.at[me], hid.at[me], h_send.at[j], h_recv.at[j], q_peer[j]))
    sent.append(send(hid.at[me], hid.at[me], k_send.at[0], k_recv.at[0], sibling))

    def down(*ms):
        return jnp.dot(jnp.concatenate([hid[m] for m in ms], axis=1),
                       jnp.concatenate([w2[pl.ds(pl.multiple_of(m * part, part), part), :] for m in ms], axis=0),
                       preferred_element_type=F32)

    theirs = (1 - core) * zhi
    for j in order[:-1][::-1]:
        came = core * zhi + lax.rem(zh + zhi - j, zhi)
        arrived(hid.at[came], h_send.at[j], h_recv.at[j], q_peer[j])
        sent.append(send(hid.at[came], hid.at[came], k_send.at[j], k_recv.at[j], sibling))
    result = None
    for j in order[::-1]:
        q = lax.rem(zh + zhi - j, zhi)
        arrived(hid.at[theirs + q], k_send.at[j], k_recv.at[j], sibling)
        more = down(core * zhi + q, theirs + q)
        result = more if result is None else result + more
    result = (result * wcol[:, 0:1]).astype(BF16)

    def spread(t):
        acc[pl.ds(pl.multiple_of(t * block, block), block), :] = jnp.dot(
            sel_t[t], result, preferred_element_type=F32).astype(BF16)

    def take_in(w, direction, c, d, onto):
        for e, p in from_(direction, c).items():
            if p == d:
                arrived(rbuf.at[w, c, e - 1], r_send.at[w, c, e - 1], r_recv.at[w, c, e - 1], s_to(direction))
                onto += rbuf[w, c, e - 1].astype(F32)
        return onto

    def pass_on(w, direction, c, d):
        of = at_chunk(lax.rem(s + n - direction * d, n), c)
        p = from_(direction, c)[d]
        if d in from_(direction, c).values():
            acc[of, :] = take_in(w, direction, c, d, acc[of, :].astype(F32)).astype(BF16)
        sent.append(send(acc.at[of], rbuf.at[w, c, d - 1], r_send.at[w, c, d - 1], r_recv.at[w, c, d - 1],
                         s_to(-direction * (d - p))))

    for d in range(n // 2, 0, -1):
        spread(lax.rem(s + d, n))
        if d < n // 2:
            spread(lax.rem(s + n - d, n))
        for w, direction, c in ways:
            if d <= hops(direction, c) and d not in from_(direction, c).values():
                pass_on(w, direction, c, d)
    spread(s)
    for d in range(n // 2, 0, -1):
        for w, direction, c in ways:
            if d <= hops(direction, c) and d in from_(direction, c).values():
                pass_on(w, direction, c, d)
    for c in range(CHUNKS):
        summed = acc[at_chunk(s, c), :].astype(F32)
        for w, direction in enumerate((1, -1)):
            summed = take_in(w, direction, c, 0, summed)
        tot[c * chunk:(c + 1) * chunk, :] = summed

    fsend[...] = fold(tot[...].reshape(2 * n, rows, feat)).astype(BF16)
    for m, (k, dz) in enumerate(near):
        to = lax.rem(f + k, n) * 2 + other_z(dz)
        sent.append(send(fsend.at[to], frecv.at[m], g_send.at[m], g_recv.at[m], f_peer[k, dz]))
    summed = jnp.zeros((2 * rows, feat // 2), F32)
    for m, (k, dz) in enumerate(near):
        arrived(frecv.at[m], g_send.at[m], g_recv.at[m], f_peer[k, dz])
        summed += frecv[m].astype(F32)
    own8 = tot[pl.ds(pl.multiple_of(mine2 * rows, rows), rows), :]
    out_ref[...] = (own8 + unfold(summed)).astype(out_ref.dtype)

    for copy in sent:
        copy.wait_send()


def on_device(n, zhi, tokens, expert_ids, route_weight, owner, gate_weight, up_weight, down_weight):
    rows, feat = tokens.shape
    total_rows = expert_ids.shape[0]
    ff = gate_weight.shape[2]
    part = ff // 2 // zhi
    cap = min(20 * rows, total_rows)
    pair = 2 * rows
    block = n * pair
    chunk = block // CHUNKS
    half_ring = max(n // 2, 1)
    dma = pltpu.SemaphoreType.DMA
    vmem = pl.BlockSpec(memory_space=pltpu.VMEM)
    hbm = pl.BlockSpec(memory_space=pl.ANY)
    return pl.pallas_call(
        functools.partial(kernel, n, zhi, cap, TREE),
        out_shape=jax.ShapeDtypeStruct((rows, feat), BF16),
        in_specs=[hbm] * 7,
        out_specs=vmem,
        scratch_shapes=[
            pltpu.VMEM(expert_ids.shape[::-1], I32),
            pltpu.VMEM(route_weight.shape[::-1], F32),
            pltpu.VMEM((1, owner.shape[0]), I32),
            pltpu.VMEM((rows, feat), BF16),
            pltpu.VMEM((2, feat, ff), BF16),
            pltpu.VMEM((ff, feat), BF16),
            pltpu.VMEM((2 * n, pair, feat // 2), BF16),
            pltpu.VMEM((total_rows, feat), BF16),
            pltpu.VMEM((n, cap, block), BF16),
            pltpu.VMEM((n, block, cap), BF16),
            pltpu.VMEM((cap, 128), F32),
            pltpu.VMEM((2 * zhi, cap, part), BF16),
            pltpu.VMEM((zhi, cap, 2 * part), F32),
            pltpu.VMEM((zhi, cap, 2 * part), F32),
            pltpu.VMEM((zhi, cap, 2 * part), BF16),
            pltpu.VMEM((zhi, cap, 2 * part), BF16),
            pltpu.VMEM((total_rows, feat), BF16),
            pltpu.VMEM((2, CHUNKS, half_ring, chunk, feat), BF16),
            pltpu.VMEM((block, feat), F32),
            pltpu.VMEM((2 * n, pair, feat // 2), BF16),
            pltpu.VMEM((2 * n - 1, pair, feat // 2), BF16),
            dma((4,)), dma((2,)), dma,
            dma((2 * n - 1,)), dma((2 * n - 1,)),
            dma((2, CHUNKS, half_ring)), dma((2, CHUNKS, half_ring)),
            dma((zhi,)), dma((zhi,)),
            dma((zhi,)), dma((zhi,)),
            dma((zhi,)), dma((zhi,)),
            dma((zhi,)), dma((zhi,)),
            dma((2, CHUNKS, half_ring)), dma((2, CHUNKS, half_ring)),
            dma((2 * n - 1,)), dma((2 * n - 1,)),
        ],
        compiler_params=pltpu.CompilerParams(
            collective_id=0, has_side_effects=True, vmem_limit_bytes=55216 * 1024
        ),
        cost_estimate=pl.CostEstimate(flops=2 * cap * feat * ff * 3, bytes_accessed=6 * feat * ff,
                                      transcendentals=cap * ff // 8),
    )(expert_ids.T, route_weight.T, owner.reshape(1, -1), tokens, gate_weight, up_weight, down_weight)


def solution(mesh):
    n = math.isqrt(mesh.shape["grp"] // 2)
    return jax.shard_map(
        functools.partial(on_device, n, mesh.shape["tp"] // 2),
        mesh=mesh,
        in_specs=(
            P("grp", "tp"),
            P(),
            P(),
            P(),
            P("grp", "tp", None),
            P("grp", "tp", None),
            P("grp", None, "tp"),
        ),
        out_specs=P("grp", "tp"),
        check_vma=False,
    )
```

```python
import functools
import math

import jax
import jax.numpy as jnp
from jax import lax
from jax.experimental import pallas as pl
from jax.experimental.pallas import tpu as pltpu
from jax.sharding import PartitionSpec as P

BF16, F32, I32 = jnp.bfloat16, jnp.float32, jnp.int32
MESH = pl.DeviceIdType.MESH


TREE = "two"
CHUNKS = 4


def parents(tree, length):
    if tree == "ring":
        return {d: d - 1 for d in range(1, length + 1)}
    if tree == "direct":
        return {d: 0 for d in range(1, length + 1)}
    return {d: 0 if d <= 2 else 2 for d in range(1, length + 1)}


def kernel(n, zhi, cap, tree, ids_hbm, rw_hbm, owner_hbm, tok_hbm, gate_ref, up_ref, down_ref, out_ref,
           ids_ref, rw_ref, owner_ref, tok_ref, w1, w2, stage, tok, sel, sel_t, wcol, hid, psend, precv, zsend, zrecv, acc, rbuf, tot, fsend, frecv,
           i_sem, w_sem, d_sem, f_send, f_recv, s_send, s_recv, c_send, c_recv, q_send, q_recv,
           h_send, h_recv, k_send, k_recv, r_send, r_recv, g_send, g_recv):
    rows, feat = tok_ref.shape
    ff = down_ref.shape[1]
    half = ff // 2
    part = half // zhi
    pair = 2 * rows
    block = n * pair
    chunk = block // CHUNKS
    total_rows = n * block
    grp, tp = lax.axis_index("grp"), lax.axis_index("tp")
    x, zlo, y = lax.rem(grp, n), lax.rem(lax.div(grp, n), 2), lax.div(grp, 2 * n)
    zh, core = lax.div(tp, 2), lax.rem(tp, 2)
    turn = core
    f = x * (1 - turn) + y * turn
    s = y * (1 - turn) + x * turn

    def at(f_, s_, z_):
        y_ = s_ * (1 - turn) + f_ * turn
        x_ = f_ * (1 - turn) + s_ * turn
        return ((y_ * 2 + z_) * n + x_, tp)

    def other_z(dz):
        return zlo + dz - 2 * zlo * dz

    near = sorted([(k, dz) for k in range(n) for dz in range(2)][1:], key=lambda v: -min(v[0], n - v[0]) - v[1])
    f_peer = {(k, dz): at(lax.rem(f + k, n), s, other_z(dz)) for k, dz in near}
    ways = [(w, direction, c) for c in range(CHUNKS) for w, direction in enumerate((1, -1))]

    def hops(direction, c):
        return n // 2 if (direction > 0) == (c % 2 == 0) else n // 2 - 1

    def from_(direction, c):
        return parents(tree, hops(direction, c))

    steps = sorted({d - p for w, direction, c in ways for d, p in from_(direction, c).items()})
    s_peer = {sign * d: at(f, lax.rem(s + n + sign * d, n), zlo) for d in steps for sign in (1, -1)}
    if 2 * max(steps) == n:
        del s_peer[-max(steps)]

    def s_to(d):
        return s_peer[d] if d in s_peer else s_peer[-d]

    sibling = (grp, zh * 2 + (1 - core))
    q_peer = [None] + [(grp, lax.rem(zh + j, zhi) * 2 + core) for j in range(1, zhi)]

    def send(src, dst, ssem, rsem, device):
        copy = pltpu.make_async_remote_copy(src_ref=src, dst_ref=dst, send_sem=ssem, recv_sem=rsem,
                                            device_id=device, device_id_type=MESH)
        copy.start()
        return copy

    def arrived(dst, ssem, rsem, device):
        pltpu.make_async_remote_copy(src_ref=dst, dst_ref=dst, send_sem=ssem, recv_sem=rsem,
                                     device_id=device, device_id_type=MESH).wait_recv()

    sent = []

    def load(src, dst, sem):
        copy = pltpu.make_async_copy(src, dst, sem)
        copy.start()
        return copy

    rows_in = load(tok_hbm, tok_ref, i_sem.at[0])
    peers = list(f_peer.values()) + list(s_peer.values()) + q_peer[1:] + [sibling]
    barrier = pltpu.get_barrier_semaphore()
    for peer in peers:
        pl.semaphore_signal(barrier, inc=1, device_id=peer, device_id_type=MESH)

    def fold(v):
        return jnp.concatenate([v[..., :feat // 2], v[..., feat // 2:]], axis=-2)

    def unfold(v):
        return jnp.concatenate([v[..., :rows, :], v[..., rows:, :]], axis=-1)

    mine2 = f * 2 + zlo
    rows_in.wait()
    stage[mine2] = fold(tok_ref[...].astype(F32)).astype(BF16)
    pl.semaphore_wait(barrier, len(peers))
    for m, (k, dz) in enumerate(near):
        sent.append(send(stage.at[mine2], stage.at[mine2], f_send.at[m], f_recv.at[m], f_peer[k, dz]))

    small = [load(ids_hbm, ids_ref, i_sem.at[1]), load(rw_hbm, rw_ref, i_sem.at[2]),
             load(owner_hbm, owner_ref, i_sem.at[3])]
    loads = [load(gate_ref.at[0], w1.at[0], w_sem.at[0]), load(up_ref.at[0], w1.at[1], w_sem.at[1])]
    load_down = load(down_ref.at[0], w2, d_sem)
    for copy in small:
        copy.wait()

    experts = owner_ref.shape[1]
    mine = jnp.sum(jnp.where(owner_ref[...] == grp, lax.broadcasted_iota(I32, (1, experts), 1), 0),
                   axis=1, keepdims=True)
    hit = ids_ref[...] == mine
    taken = jnp.max(jnp.where(hit, 1.0, 0.0), axis=0, keepdims=True)
    weight = jnp.sum(jnp.where(hit, rw_ref[...], 0.0), axis=0, keepdims=True)
    high = weight.astype(BF16).astype(F32)
    middle = (weight - high).astype(BF16).astype(F32)
    low = weight - high - middle
    lanes = block

    def square(v):
        wide = jnp.broadcast_to(v, (n, total_rows))
        at_row = lax.broadcasted_iota(I32, (n, lanes), 0)
        return sum(jnp.where(at_row == a, wide[:, a * lanes:(a + 1) * lanes], 0.0) for a in range(n))

    taken_sq = square(taken)
    before = jnp.where(lax.broadcasted_iota(I32, (lanes, lanes), 0) < lax.broadcasted_iota(I32, (lanes, lanes), 1),
                       1.0, 0.0).astype(BF16)
    in_line = jnp.dot(taken_sq.astype(BF16), before, preferred_element_type=F32)
    counts = jnp.sum(taken_sq, axis=1, keepdims=True)
    ahead = jnp.zeros((n, lanes), F32)
    at_row = lax.broadcasted_iota(I32, (n, lanes), 0)
    for a in range(n - 1):
        ahead += jnp.where(at_row > a, counts[a:a + 1, :], 0.0)
    place_sq = jnp.where(taken_sq > 0.5, in_line + ahead, -1.0)
    stacked = jnp.concatenate([place_sq, square(high), square(middle), square(low)], axis=0).astype(BF16)
    position = lax.broadcasted_iota(I32, (1, total_rows), 1)
    bits = [int(math.log2(v)) for v in (rows, n)]
    i_ = position & (rows - 1)
    z_ = lax.shift_right_logical(position, bits[0]) & 1
    f_ = lax.shift_right_logical(position, bits[0] + 1) & (n - 1)
    s_ = lax.shift_right_logical(position, bits[0] + 1 + bits[1])
    y_ = s_ * (1 - turn) + f_ * turn
    x_ = f_ * (1 - turn) + s_ * turn
    lane_of = (z_ * n + x_) * rows + i_
    take = jnp.where(lax.broadcasted_iota(I32, (lanes, total_rows), 0) == lane_of, 1.0, 0.0).astype(BF16)
    spread_out = jnp.dot(stacked, take, preferred_element_type=F32)
    keep = lax.broadcasted_iota(I32, (n, total_rows), 0) == y_

    def line(m):
        return jnp.sum(jnp.where(keep, spread_out[m * n:(m + 1) * n], 0.0), axis=0, keepdims=True)

    place_of = line(0)
    weight_at = line(1) + line(2) + line(3)
    slot_at = lax.broadcasted_iota(I32, (cap, block), 0).astype(F32)
    weights = jnp.zeros((cap, block), F32)
    for t in range(n):
        here = slice(t * block, (t + 1) * block)
        one = jnp.where(place_of[:, here] == slot_at, 1.0, 0.0)
        sel[t] = one.astype(BF16)
        weights += one * weight_at[:, here]
    wcol[...] = jnp.broadcast_to(jnp.sum(weights, axis=1, keepdims=True), wcol.shape)

    for m, (k, dz) in enumerate(near):
        came = lax.rem(f + n - k, n) * 2 + other_z(dz)
        arrived(stage.at[came], f_send.at[m], f_recv.at[m], f_peer[k, dz])
    tok[pl.ds(pl.multiple_of(s * block, block), block), :] = (
        unfold(stage[...].astype(F32)).reshape(block, feat).astype(BF16))

    def whole(direction, c, e):
        tree_ = from_(direction, c)
        return tree_.get(e) == 0 and e not in tree_.values() and 2 * e < n - 2

    def piece(s_, direction, c, e):
        if whole(direction, c, e):
            return pl.ds(pl.multiple_of(s_ * block, block), block)
        return at_chunk(s_, c)

    def at_chunk(s_, c):
        return pl.ds(pl.multiple_of(s_ * block + c * chunk, chunk), chunk)

    order_out = sorted(range(1, n // 2 + 1), key=lambda d: (d not in parents(tree, n // 2).values(), -d))

    def hand_out(d, those):
        for e in order_out:
            for w, direction, c in those:
                if from_(direction, c).get(e) == d and not (c and whole(direction, c, e)):
                    held = piece(lax.rem(s + n - direction * d, n), direction, c, e)
                    sent.append(send(tok.at[held], tok.at[held], s_send.at[w, c, e - 1], s_recv.at[w, c, e - 1],
                                     s_to(direction * (e - d))))

    hand_out(0, ways)

    def rows_of(*ts):
        return jnp.dot(jnp.concatenate([sel[t] for t in ts], axis=1),
                       jnp.concatenate([tok[pl.ds(pl.multiple_of(t * block, block), block), :] for t in ts], axis=0),
                       preferred_element_type=F32)

    picked = None
    for h in sorted(range(1, n // 2 + 1), key=lambda d: (d not in parents(tree, n // 2).values(), d)):
        for w, direction, c in ways:
            if h <= hops(direction, c) and not (c and whole(direction, c, h)):
                came = piece(lax.rem(s + n - direction * h, n), direction, c, h)
                arrived(tok.at[came], s_send.at[w, c, h - 1], s_recv.at[w, c, h - 1], s_to(direction))
                hand_out(h, [(w, direction, c)])
        more = rows_of(lax.rem(s + h, n), s if h == n // 2 else lax.rem(s + n - h, n))
        picked = more if picked is None else picked + more
    rows_x = picked.astype(BF16)

    for copy in loads:
        copy.wait()
    order = [1] if zhi == 2 else [2, 1, 3]
    order = order + [0]

    def partial(side, j):
        columns = pl.ds(pl.multiple_of(side * half + lax.rem(zh + j, zhi) * part, part), part)
        return jnp.dot(rows_x, jnp.concatenate([w1[0, :, columns], w1[1, :, columns]], axis=1),
                       preferred_element_type=F32)

    def for_sibling(j):
        psend[j] = partial(1 - core, j)
        sent.append(send(psend.at[j], precv.at[j], c_send.at[j], c_recv.at[j], sibling))

    own = None
    for_sibling(order[0])
    for m, j in enumerate(order):
        if m + 1 < zhi:
            for_sibling(order[m + 1])
        product = partial(core, j)
        arrived(precv.at[j], c_send.at[j], c_recv.at[j], sibling)
        both = product + precv[j]
        if j == 0:
            own = both
        else:
            zsend[j] = both.astype(BF16)
            sent.append(send(zsend.at[j], zrecv.at[j], q_send.at[j], q_recv.at[j], q_peer[j]))

    for t in range(n):
        sel_t[t] = sel[t].astype(F32).T.astype(BF16)
    load_down.wait()
    for j in order[:-1][::-1]:
        arrived(zrecv.at[j], q_send.at[j], q_recv.at[j], q_peer[j])
        own += zrecv[j].astype(F32)
    gate, up = own[:, :part], own[:, part:]
    me = core * zhi + zh
    hid[me] = (gate / (1.0 + jnp.exp(-gate)) * up).astype(BF16)

    for j in order[:-1]:
        sent.append(send(hid.at[me], hid.at[me], h_send.at[j], h_recv.at[j], q_peer[j]))
    sent.append(send(hid.at[me], hid.at[me], k_send.at[0], k_recv.at[0], sibling))

    def down(*ms):
        return jnp.dot(jnp.concatenate([hid[m] for m in ms], axis=1),
                       jnp.concatenate([w2[pl.ds(pl.multiple_of(m * part, part), part), :] for m in ms], axis=0),
                       preferred_element_type=F32)

    theirs = (1 - core) * zhi
    for j in order[:-1][::-1]:
        came = core * zhi + lax.rem(zh + zhi - j, zhi)
        arrived(hid.at[came], h_send.at[j], h_recv.at[j], q_peer[j])
        sent.append(send(hid.at[came], hid.at[came], k_send.at[j], k_recv.at[j], sibling))
    result = None
    for j in order[::-1]:
        q = lax.rem(zh + zhi - j, zhi)
        arrived(hid.at[theirs + q], k_send.at[j], k_recv.at[j], sibling)
        more = down(core * zhi + q, theirs + q)
        result = more if result is None else result + more
    result = (result * wcol[:, 0:1]).astype(BF16)

    def spread(t):
        acc[pl.ds(pl.multiple_of(t * block, block), block), :] = jnp.dot(
            sel_t[t], result, preferred_element_type=F32).astype(BF16)

    def landing(direction, c, e):
        return pl.ds(0, block) if whole(direction, c, e) else pl.ds(c * chunk, chunk)

    def take_in(w, direction, c, d, onto):
        for e, p in from_(direction, c).items():
            if p == d:
                if not (c and whole(direction, c, e)):
                    arrived(rbuf.at[w, e - 1, landing(direction, c, e)], r_send.at[w, c, e - 1],
                            r_recv.at[w, c, e - 1], s_to(direction))
                onto += rbuf[w, e - 1, c * chunk:(c + 1) * chunk].astype(F32)
        return onto

    def pass_on(w, direction, c, d):
        if c and whole(direction, c, d):
            return
        of = piece(lax.rem(s + n - direction * d, n), direction, c, d)
        p = from_(direction, c)[d]
        if d in from_(direction, c).values():
            acc[of, :] = take_in(w, direction, c, d, acc[of, :].astype(F32)).astype(BF16)
        sent.append(send(acc.at[of], rbuf.at[w, d - 1, landing(direction, c, d)], r_send.at[w, c, d - 1],
                         r_recv.at[w, c, d - 1], s_to(-direction * (d - p))))

    for d in range(n // 2, 0, -1):
        spread(lax.rem(s + d, n))
        if d < n // 2:
            spread(lax.rem(s + n - d, n))
        for w, direction, c in ways:
            if d <= hops(direction, c) and d not in from_(direction, c).values():
                pass_on(w, direction, c, d)
    spread(s)
    for d in range(n // 2, 0, -1):
        for w, direction, c in ways:
            if d <= hops(direction, c) and d in from_(direction, c).values():
                pass_on(w, direction, c, d)
    for c in range(CHUNKS):
        summed = acc[at_chunk(s, c), :].astype(F32)
        for w, direction in enumerate((1, -1)):
            summed = take_in(w, direction, c, 0, summed)
        tot[c * chunk:(c + 1) * chunk, :] = summed

    fsend[...] = fold(tot[...].reshape(2 * n, rows, feat)).astype(BF16)
    for m, (k, dz) in enumerate(near):
        to = lax.rem(f + k, n) * 2 + other_z(dz)
        sent.append(send(fsend.at[to], frecv.at[m], g_send.at[m], g_recv.at[m], f_peer[k, dz]))
    summed = jnp.zeros((2 * rows, feat // 2), F32)
    for m, (k, dz) in enumerate(near):
        arrived(frecv.at[m], g_send.at[m], g_recv.at[m], f_peer[k, dz])
        summed += frecv[m].astype(F32)
    own8 = tot[pl.ds(pl.multiple_of(mine2 * rows, rows), rows), :]
    out_ref[...] = (own8 + unfold(summed)).astype(out_ref.dtype)

    for copy in sent:
        copy.wait_send()


def on_device(n, zhi, tokens, expert_ids, route_weight, owner, gate_weight, up_weight, down_weight):
    rows, feat = tokens.shape
    total_rows = expert_ids.shape[0]
    ff = gate_weight.shape[2]
    part = ff // 2 // zhi
    cap = min(20 * rows, total_rows)
    pair = 2 * rows
    block = n * pair
    chunk = block // CHUNKS
    half_ring = max(n // 2, 1)
    dma = pltpu.SemaphoreType.DMA
    vmem = pl.BlockSpec(memory_space=pltpu.VMEM)
    hbm = pl.BlockSpec(memory_space=pl.ANY)
    return pl.pallas_call(
        functools.partial(kernel, n, zhi, cap, TREE),
        out_shape=jax.ShapeDtypeStruct((rows, feat), BF16),
        in_specs=[hbm] * 7,
        out_specs=vmem,
        scratch_shapes=[
            pltpu.VMEM(expert_ids.shape[::-1], I32),
            pltpu.VMEM(route_weight.shape[::-1], F32),
            pltpu.VMEM((1, owner.shape[0]), I32),
            pltpu.VMEM((rows, feat), BF16),
            pltpu.VMEM((2, feat, ff), BF16),
            pltpu.VMEM((ff, feat), BF16),
            pltpu.VMEM((2 * n, pair, feat // 2), BF16),
            pltpu.VMEM((total_rows, feat), BF16),
            pltpu.VMEM((n, cap, block), BF16),
            pltpu.VMEM((n, block, cap), BF16),
            pltpu.VMEM((cap, 128), F32),
            pltpu.VMEM((2 * zhi, cap, part), BF16),
            pltpu.VMEM((zhi, cap, 2 * part), F32),
            pltpu.VMEM((zhi, cap, 2 * part), F32),
            pltpu.VMEM((zhi, cap, 2 * part), BF16),
            pltpu.VMEM((zhi, cap, 2 * part), BF16),
            pltpu.VMEM((total_rows, feat), BF16),
            pltpu.VMEM((2, half_ring, block, feat), BF16),
            pltpu.VMEM((block, feat), F32),
            pltpu.VMEM((2 * n, pair, feat // 2), BF16),
            pltpu.VMEM((2 * n - 1, pair, feat // 2), BF16),
            dma((4,)), dma((2,)), dma,
            dma((2 * n - 1,)), dma((2 * n - 1,)),
            dma((2, CHUNKS, half_ring)), dma((2, CHUNKS, half_ring)),
            dma((zhi,)), dma((zhi,)),
            dma((zhi,)), dma((zhi,)),
            dma((zhi,)), dma((zhi,)),
            dma((zhi,)), dma((zhi,)),
            dma((2, CHUNKS, half_ring)), dma((2, CHUNKS, half_ring)),
            dma((2 * n - 1,)), dma((2 * n - 1,)),
        ],
        compiler_params=pltpu.CompilerParams(
            collective_id=0, has_side_effects=True, vmem_limit_bytes=55216 * 1024
        ),
        cost_estimate=pl.CostEstimate(flops=2 * cap * feat * ff * 3, bytes_accessed=6 * feat * ff,
                                      transcendentals=cap * ff // 8),
    )(expert_ids.T, route_weight.T, owner.reshape(1, -1), tokens, gate_weight, up_weight, down_weight)


def solution(mesh):
    n = math.isqrt(mesh.shape["grp"] // 2)
    return jax.shard_map(
        functools.partial(on_device, n, mesh.shape["tp"] // 2),
        mesh=mesh,
        in_specs=(
            P("grp", "tp"),
            P(),
            P(),
            P(),
            P("grp", "tp", None),
            P("grp", "tp", None),
            P("grp", None, "tp"),
        ),
        out_specs=P("grp", "tp"),
        check_vma=False,
    )
```
